512 devices in a mesh: rep: 16 (over x_hi, y, core), fsdp: 32 (over z, x_lo).
Axes of the slice: x: 4 (x_hi: 2, x_lo: 2; x = x_hi * 2 + x_lo), y: 4, z: 16, core: 2. Of those that a mesh axis runs over, the one named last changes fastest.
Arguments:
- weights: bfloat16 [6, 6144, 1024], P(None, 'fsdp'), may hold values from -0.078125 to 0.078125
- momentum: bfloat16 [6144, 1024], P('fsdp'), may hold values from -0.023925781 to 0.023925781
- pseudo_grad: bfloat16 [16, 6144, 1024], P('rep', 'fsdp'), may hold values from -0.078125 to 0.078125
- tokens: bfloat16 [65536, 6144], P(('rep', 'fsdp')), may hold values from -6 to 6
- fragment: int32 [6], replicated, may hold values from 0 to 5, each once
Outputs:
- new_weights: bfloat16 [16, 6144, 1024], P('rep', 'fsdp')
- new_momentum: bfloat16 [6144, 1024], P('fsdp')
- layer_out: bfloat16 [65536, 1024], P(('rep', 'fsdp'))
The draws below stay inside these ranges and needn't reach their ends.
Inputs may be any that keep to these rules, and one draw needn't show every extreme that they name: fragment holds each of the 6 layer indices once.
All inputs are finite; a program needn't handle non-finite values.
Results may differ from the reference program's by a relative error of at most 0.017.
Values may be sent and summed in bfloat16 or wider, within the bound.
No kernel may reach another device: no remote copies, remote signals or barrier semaphores. Data moves between devices by JAX's collectives and lax.ppermute only.
A program may use at most 64 MiB of HBM per device.

```python
import jax
import jax.numpy as jnp
from jax import lax

D = 6144
COLS = 1024
LAYERS = 6
TOKENS = 65536
N_REP = 16


def block_scale(key, shape, split, low, top_value):
    factor_of, own = 1.0, jax.random.fold_in(key, 6)
    for position, shards_of in split:
        heights = jnp.exp(jax.random.uniform(jax.random.fold_in(own, position), (shards_of,), jnp.float32, low / len(split), top_value / len(split)))
        factor_of = factor_of * jnp.repeat(heights, shape[position] // shards_of).reshape([-1 if axis == position else 1 for axis in range(len(shape))])
    return factor_of


def bell_draw(key, dims, width, most, shards=(), kind=jnp.bfloat16):
    entries = width * jax.random.normal(key, dims, jnp.float32)
    if shards:
        entries = entries * block_scale(key, dims, shards, -0.22, 0.18)
    return jnp.clip(entries, -most, most).astype(kind)


def setup_inputs(seed: int = 0) -> dict:
    keys = jax.random.split(jax.random.key(seed), 6)
    weights = bell_draw(keys[0], (LAYERS, D, COLS), D ** -0.5, 0.078125, ((1, 32),))
    momentum = bell_draw(keys[1], (D, COLS), 0.004, 0.023925781, ((0, 32),))
    pseudo_grad = bell_draw(keys[2], (N_REP, D, COLS), D ** -0.5, 0.078125, ((0, 16), (1, 32)))
    tokens = bell_draw(keys[3], (TOKENS, D), 1.0, 6.0, ((0, 512),))
    fragment = jax.random.permutation(keys[4], LAYERS).astype(jnp.int32)
    return dict(weights=weights, momentum=momentum, pseudo_grad=pseudo_grad, tokens=tokens, fragment=fragment)


MU = 0.9
OUTER_LR = 0.7
MIX = 0.5


def reference(weights, momentum, pseudo_grad, tokens, fragment):
    index = fragment[0].astype(jnp.int32)
    second = fragment[1].astype(jnp.int32)
    synced = lax.dynamic_index_in_dim(weights, index, 0, keepdims=False).astype(jnp.float32)
    following = lax.dynamic_index_in_dim(weights, second, 0, keepdims=False)
    averaged = jnp.sum(pseudo_grad.astype(jnp.float32), axis=0) / N_REP
    velocity = MU * momentum.astype(jnp.float32) + averaged
    outer_weights = synced - OUTER_LR * (averaged + MU * velocity)
    inner_weights = synced[None] - pseudo_grad.astype(jnp.float32)
    new_weights = (MIX * inner_weights + (1.0 - MIX) * outer_weights[None]).astype(jnp.bfloat16)
    layer_out = jnp.dot(tokens, following, preferred_element_type=jnp.float32).astype(jnp.bfloat16)
    return new_weights, velocity.astype(jnp.bfloat16), layer_out
```

```python
import jax
import jax.numpy as jnp
from jax import lax
from jax.experimental import pallas as pl
from jax.experimental.pallas import tpu as pltpu
from jax.sharding import Mesh, PartitionSpec as P

MU = 0.9
OUTER_LR = 0.7
MIX = 0.5

SIZES = {"xh": 2, "y": 4, "core": 2, "zh": 4, "zl": 4, "xl": 2}
AXES = tuple(SIZES)
REP = ("xh", "y", "core")
FSDP = ("zh", "zl", "xl")
CHIPS = 4
PARTS = 4

ANY = pl.BlockSpec(memory_space=pl.ANY)


def permute(value, move):
    pairs = []
    total = 1
    for size in SIZES.values():
        total *= size
    for source in range(total):
        rest, at = source, {}
        for axis in reversed(AXES):
            at[axis] = rest % SIZES[axis]
            rest //= SIZES[axis]
        to = move(dict(at))
        target = 0
        for axis in AXES:
            target = target * SIZES[axis] + to[axis] % SIZES[axis]
        pairs.append((source, target))
    return lax.ppermute(value, AXES, pairs)


def along_z(step):
    def move(at):
        z = (at["zh"] * SIZES["zl"] + at["zl"] + step) % (SIZES["zh"] * SIZES["zl"])
        at["zh"], at["zl"] = divmod(z, SIZES["zl"])
        return at

    return move


def in_group(step):
    def move(at):
        if at["core"] == 0:
            at["y"] = (at["y"] + step) % SIZES["y"]
        else:
            x = (at["xh"] * SIZES["xl"] + at["xl"] + step) % (SIZES["xh"] * SIZES["xl"])
            at["xh"], at["xl"] = divmod(x, SIZES["xl"])
        return at

    return move


def flip(axis, bit=1):
    def move(at):
        at[axis] ^= bit
        return at

    return move


def quarter(xl):
    return lax.rem(lax.axis_index("xh") * SIZES["xl"] + xl + lax.axis_index("y"), CHIPS)


def pick(weights, fragment):
    rows, cols = weights.shape[1:]
    width = cols // (CHIPS * SIZES["core"])

    def kernel(fragment_ref, weights_ref, own_ref, give_ref, sems):
        xl = lax.axis_index("xl")
        core = lax.axis_index("core")
        copies = []
        for n, (ref, at) in enumerate(((own_ref, xl), (give_ref, 1 - xl))):
            start = pl.multiple_of((quarter(at) * SIZES["core"] + core) * width, 128)
            source = weights_ref.at[fragment_ref[1], :, pl.ds(start, width)]
            copies.append(pltpu.make_async_copy(source, ref, sems.at[n]))
        for copy in copies:
            copy.start()
        for copy in copies:
            copy.wait()

    shape = jax.ShapeDtypeStruct((rows, width), weights.dtype)
    return pl.pallas_call(
        kernel,
        out_shape=(shape, shape),
        in_specs=[pl.BlockSpec(memory_space=pltpu.SMEM), ANY],
        out_specs=(ANY, ANY),
        scratch_shapes=[pltpu.SemaphoreType.DMA((2,))],
    )(fragment, weights)


def multiply(blocks, own, other):
    tokens, depth = blocks[0].shape
    places, steps, rows, width = own.shape

    def kernel(*refs):
        token_refs, (own_ref, other_ref) = refs[:CHIPS], refs[CHIPS : CHIPS + 2]
        out_refs, total = refs[CHIPS + 2 : -1], refs[-1]
        zl, core = lax.axis_index("zl"), lax.axis_index("core")
        step = pl.program_id(0)

        @pl.when(step == 0)
        def _():
            total[...] = jnp.zeros_like(total)

        for n, token_ref in enumerate(token_refs):
            part = None
            for place in range(places):
                weight = jnp.concatenate([own_ref[place, 0], other_ref[place, 0]], axis=1)
                start = pl.multiple_of(lax.rem(zl + place, places) * rows, 128)
                term = jnp.dot(
                    token_ref[:, pl.ds(start, rows)], weight, preferred_element_type=jnp.float32
                )
                part = term if part is None else part + term
            total[n] += part

        @pl.when(step == steps - 1)
        def _():
            mine = pl.multiple_of(core * width, 128)
            theirs = pl.multiple_of((1 - core) * width, 128)
            for n, out_ref in enumerate(out_refs):
                out_ref[:, pl.ds(mine, width)] = total[n, :, :width].astype(out_ref.dtype)
                out_ref[:, pl.ds(theirs, width)] = total[n, :, width:].astype(out_ref.dtype)

    weight_spec = pl.BlockSpec((places, 1, rows, width), lambda s: (0, s, 0, 0))
    shape = jax.ShapeDtypeStruct((tokens, 2 * width), blocks[0].dtype)
    return pl.pallas_call(
        kernel,
        grid=(steps,),
        out_shape=(shape,) * CHIPS,
        in_specs=[pl.BlockSpec((tokens, depth // steps), lambda s: (0, s))] * CHIPS + [weight_spec] * 2,
        out_specs=(pl.BlockSpec((tokens, 2 * width), lambda s: (0, 0)),) * CHIPS,
        scratch_shapes=[pltpu.VMEM((CHIPS, tokens, 2 * width), jnp.float32)],
        compiler_params=pltpu.CompilerParams(vmem_limit_bytes=32 << 20),
        cost_estimate=pl.CostEstimate(
            flops=2 * CHIPS * tokens * depth * 2 * width,
            bytes_accessed=2 * (CHIPS * tokens * depth + depth * 2 * width),
            transcendentals=0,
        ),
    )(*blocks, own, other)


def assemble(results):
    tokens, width = results[0].shape

    def kernel(*refs):
        out_ref = refs[-1]
        first = quarter(lax.axis_index("xl"))
        for n, ref in enumerate(refs[:-1]):
            start = pl.multiple_of(lax.rem(first + n, CHIPS) * width, 128)
            out_ref[:, pl.ds(start, width)] = ref[...]

    return pl.pallas_call(
        kernel,
        out_shape=jax.ShapeDtypeStruct((tokens, CHIPS * width), results[0].dtype),
        in_specs=[pl.BlockSpec(memory_space=pltpu.VMEM)] * CHIPS,
        out_specs=pl.BlockSpec(memory_space=pltpu.VMEM),
    )(*results)


def ordered(first, mine, other):
    return jnp.where(first, jnp.concatenate([mine, other]), jnp.concatenate([other, mine]))


def layer_product(weights, tokens, fragment):
    own, give = pick(weights, fragment)
    partner = permute(give, flip("xl"))
    blocks = [tokens] + [permute(tokens, in_group(step)) for step in (1, 2, 3)]
    plane = ordered(lax.axis_index("xl") == 0, own, partner)
    here = lax.all_gather(plane, "zh", axis=0, tiled=True)
    half = here.shape[0] // 2
    before = permute(here, along_z(1))
    after = permute(here, along_z(-1))
    far_low = permute(before[:half], along_z(1))
    far_high = permute(after[half:], along_z(-1))
    held = jnp.concatenate([here, after, far_low, far_high, before])
    other = permute(held, flip("core"))
    shape = (SIZES["zl"], SIZES["zh"], *plane.shape)
    outs = multiply(blocks, held.reshape(shape), other.reshape(shape))
    results = [outs[0]] + [permute(outs[step], in_group(-step)) for step in (1, 2, 3)]
    return assemble(results)


def sum_over_rep(grad):
    core = lax.axis_index("core")
    half = grad.shape[0] // 2
    mine = lax.dynamic_slice_in_dim(grad, core * half, half)
    theirs = lax.dynamic_slice_in_dim(grad, (1 - core) * half, half)

    def add(a, b):
        return (a.astype(jnp.float32) + b.astype(jnp.float32)).astype(grad.dtype)

    total = add(mine, permute(theirs, flip("core")))
    for move in (flip("xh"), flip("y"), flip("y", 2)):
        total = add(total, permute(total, move))
    return ordered(core == 0, total, permute(total, flip("core")))


def per_device(weights, momentum, pseudo_grad, tokens, fragment):
    layer_out = layer_product(weights, tokens, fragment)
    synced = lax.dynamic_index_in_dim(weights, fragment[0], 0, keepdims=False)
    replicas = lax.axis_size(REP)
    own_grad = pseudo_grad[0].astype(jnp.float32)
    averaged = sum_over_rep(pseudo_grad[0]).astype(jnp.float32) / replicas
    velocity = MU * momentum.astype(jnp.float32) + averaged
    synced_wide = synced.astype(jnp.float32)
    outer_weights = synced_wide - OUTER_LR * (averaged + MU * velocity)
    inner_weights = synced_wide - own_grad
    blended = (MIX * inner_weights + (1.0 - MIX) * outer_weights).astype(jnp.bfloat16)
    return (blended[None], velocity.astype(jnp.bfloat16), layer_out)


def solution(mesh):
    split = Mesh(mesh.devices.reshape(tuple(SIZES.values())), AXES)
    in_specs = (
        P(None, FSDP, None),
        P(FSDP, None),
        P(REP, FSDP, None),
        P(REP + FSDP, None),
        P(),
    )
    out_specs = (P(REP, FSDP, None), P(FSDP, None), P(REP + FSDP, None))
    return jax.shard_map(
        per_device, mesh=split, in_specs=in_specs, out_specs=out_specs, check_vma=False
    )
```

```python
import jax
import jax.numpy as jnp
from jax import lax
from jax.experimental import pallas as pl
from jax.experimental.pallas import tpu as pltpu
from jax.sharding import Mesh, PartitionSpec as P

MU = 0.9
OUTER_LR = 0.7
MIX = 0.5

SIZES = {"xh": 2, "y": 4, "core": 2, "zh": 4, "zl": 4, "xl": 2}
AXES = tuple(SIZES)
REP = ("xh", "y", "core")
FSDP = ("zh", "zl", "xl")
CHIPS = 4
PARTS = SIZES["zl"]

ANY = pl.BlockSpec(memory_space=pl.ANY)
WHOLE = pl.BlockSpec(memory_space=pltpu.VMEM)


def in_vmem(*values):
    return [pltpu.with_memory_space_constraint(value, pltpu.VMEM) for value in values]


def in_hbm(*values):
    return [pltpu.with_memory_space_constraint(value, pltpu.HBM) for value in values]


def vmem_like(shape, dtype=jnp.bfloat16):
    return pltpu.VMEM(shape, dtype)


SMALL = pltpu.CompilerParams(vmem_limit_bytes=1 << 20)


def permute(value, move):
    pairs = []
    total = 1
    for size in SIZES.values():
        total *= size
    for source in range(total):
        rest, at = source, {}
        for axis in reversed(AXES):
            at[axis] = rest % SIZES[axis]
            rest //= SIZES[axis]
        to = move(dict(at))
        target = 0
        for axis in AXES:
            target = target * SIZES[axis] + to[axis] % SIZES[axis]
        pairs.append((source, target))
    return lax.ppermute(value, AXES, pairs)


def along_z(step):
    def move(at):
        z = (at["zh"] * SIZES["zl"] + at["zl"] + step) % (SIZES["zh"] * SIZES["zl"])
        at["zh"], at["zl"] = divmod(z, SIZES["zl"])
        return at

    return move


def in_group(step):
    def move(at):
        if at["core"] == 0:
            at["y"] = (at["y"] + step) % SIZES["y"]
        else:
            x = (at["xh"] * SIZES["xl"] + at["xl"] + step) % (SIZES["xh"] * SIZES["xl"])
            at["xh"], at["xl"] = divmod(x, SIZES["xl"])
        return at

    return move


def flip(axis, bit=1):
    def move(at):
        at[axis] ^= bit
        return at

    return move


def quarter(xl):
    return lax.rem(lax.axis_index("xh") * SIZES["xl"] + xl + lax.axis_index("y"), CHIPS)


def pick(weights, fragment):
    rows, cols = weights.shape[1:]
    width = cols // (CHIPS * SIZES["core"])

    def kernel(fragment_ref, weights_ref, own_ref, give_ref, sems):
        xl = lax.axis_index("xl")
        core = lax.axis_index("core")
        copies = []
        for n, (ref, at) in enumerate(((own_ref, xl), (give_ref, 1 - xl))):
            start = pl.multiple_of((quarter(at) * SIZES["core"] + core) * width, 128)
            source = weights_ref.at[fragment_ref[1], :, pl.ds(start, width)]
            copies.append(pltpu.make_async_copy(source, ref, sems.at[n]))
        for copy in copies:
            copy.start()
        for copy in copies:
            copy.wait()

    return pl.pallas_call(
        kernel,
        out_shape=[vmem_like((rows, width))] * 2,
        in_specs=[pl.BlockSpec(memory_space=pltpu.SMEM), ANY],
        out_specs=[WHOLE] * 2,
        scratch_shapes=[pltpu.SemaphoreType.DMA((2,))],
        compiler_params=SMALL,
    )(fragment, *in_hbm(weights))


def lay(own, partner):
    rows, width = own.shape

    def kernel(own_ref, partner_ref, out_ref):
        xl = lax.axis_index("xl")
        for ref, at in ((own_ref, xl), (partner_ref, 1 - xl)):
            out_ref[pl.ds(pl.multiple_of(at * rows, 16), rows), :] = ref[...]

    return pl.pallas_call(
        kernel,
        out_shape=vmem_like((2 * rows, width)),
        in_specs=[WHOLE] * 2,
        out_specs=WHOLE,
        compiler_params=SMALL,
    )(*in_vmem(own, partner))


def gate(values, after):
    def kernel(*refs):
        del refs

    return pl.pallas_call(
        kernel,
        out_shape=[vmem_like(value.shape) for value in values],
        in_specs=[WHOLE] * len(values) + [ANY] * len(after),
        out_specs=[WHOLE] * len(values),
        input_output_aliases={n: n for n in range(len(values))},
        compiler_params=SMALL,
    )(*in_vmem(*values), *after)


def column_blocks(shape, rows, width):
    for n in range(shape[1] // width):
        place, start = divmod(n * shape[0], rows)
        yield n * width, place, start


def pack(planes, grad, other, after):
    halves, steps, rows, width = planes.shape

    def kernel(planes_ref, grad_ref, other_ref, *refs):
        out_ref, entry_ref = refs[-2:]
        out_ref[:halves] = planes_ref[...]
        entry_ref[...] = planes_ref[lax.axis_index("core")]
        for column, place, start in column_blocks(grad.shape, rows, width):
            columns = pl.ds(column, width)
            total = grad_ref[:, columns].astype(jnp.float32) + other_ref[:, columns].astype(jnp.float32)
            out_ref[halves, place, pl.ds(start, grad.shape[0]), :] = total.astype(grad.dtype)

    return pl.pallas_call(
        kernel,
        out_shape=[
            jax.ShapeDtypeStruct((halves + 1, *planes.shape[1:]), planes.dtype),
            vmem_like(planes.shape[1:]),
        ],
        in_specs=[WHOLE] * 3 + [ANY] * len(after),
        out_specs=[WHOLE] * 2,
        compiler_params=pltpu.CompilerParams(vmem_limit_bytes=4 << 20),
    )(*in_vmem(planes, grad, other), *after)


def unpack(mine, theirs, shape):
    behind = mine.shape[0] - 1
    rows, width = mine.shape[2:]

    def kernel(mine_ref, theirs_ref, out_ref):
        for column, place, start in column_blocks(shape, rows, width):
            block = (0, place, pl.ds(start, shape[0]), slice(None))
            total = mine_ref[block].astype(jnp.float32) + theirs_ref[block].astype(jnp.float32)
            out_ref[:, pl.ds(column, width)] = total.astype(out_ref.dtype)

    spec = pl.BlockSpec((1, *mine.shape[1:]), lambda n: (behind, 0, 0, 0))
    return pl.pallas_call(
        kernel,
        grid=(1,),
        out_shape=vmem_like(shape),
        in_specs=[spec] * 2,
        out_specs=WHOLE,
        compiler_params=pltpu.CompilerParams(vmem_limit_bytes=4 << 20),
    )(mine, theirs)


def multiply(blocks, here, mine, theirs, far):
    tokens, depth = blocks[0].shape
    halves, steps, rows, width = here.shape

    def kernel(*refs):
        token_refs, (here_ref, mine_ref, theirs_ref, far_ref) = refs[:CHIPS], refs[CHIPS : CHIPS + 4]
        out_refs, total = refs[CHIPS + 4 : -1], refs[-1]
        zl, core = lax.axis_index("zl"), lax.axis_index("core")
        step = pl.program_id(0)
        sets = ((here_ref, 0), (mine_ref, 3 - 2 * core), (theirs_ref, 1 + 2 * core), (far_ref, 2))
        for n, token_ref in enumerate(token_refs):
            part = None
            for ref, place in sets:
                weight = jnp.concatenate([ref[half, 0] for half in range(halves)], axis=1)
                plane = lax.rem(zl + place, PARTS)
                if n == 0:
                    plane += step * PARTS
                start = pl.multiple_of(plane * rows, 128)
                term = jnp.dot(
                    token_ref[:, pl.ds(start, rows)], weight, preferred_element_type=jnp.float32
                )
                part = term if part is None else part + term
            total[n] = jnp.where(step == 0, part, total[n] + part)

        @pl.when(step == steps - 1)
        def _():
            for n, out_ref in enumerate(out_refs):
                out_ref[...] = total[n].astype(out_ref.dtype)

    weight_spec = pl.BlockSpec((halves, 1, rows, width), lambda s: (0, s, 0, 0))
    token_spec = pl.BlockSpec((tokens, depth // steps), lambda s: (0, s))
    shape = (tokens, halves * width)
    return pl.pallas_call(
        kernel,
        grid=(steps,),
        out_shape=(vmem_like(shape),) * CHIPS,
        in_specs=[WHOLE] + [token_spec] * (CHIPS - 1) + [weight_spec] * 4,
        out_specs=(WHOLE,) * CHIPS,
        scratch_shapes=[pltpu.VMEM((CHIPS, *shape), jnp.float32)],
        compiler_params=pltpu.CompilerParams(vmem_limit_bytes=32 << 20),
        cost_estimate=pl.CostEstimate(
            flops=2 * CHIPS * tokens * depth * halves * width,
            bytes_accessed=2 * (CHIPS * tokens + halves * width) * depth,
            transcendentals=0,
        ),
    )(*in_vmem(blocks[0]), *blocks[1:], here, mine, theirs, far)


def assemble(results, after):
    tokens, width = results[0].shape

    def kernel(*refs):
        out_ref = refs[-1]
        first = quarter(lax.axis_index("xl"))
        for n, ref in enumerate(refs[:CHIPS]):
            start = pl.multiple_of(lax.rem(first + n, CHIPS) * width, 128)
            out_ref[:, pl.ds(start, width)] = ref[...]

    return pl.pallas_call(
        kernel,
        out_shape=jax.ShapeDtypeStruct((tokens, CHIPS * width), results[0].dtype),
        in_specs=[WHOLE] * CHIPS + [ANY],
        out_specs=WHOLE,
        compiler_params=pltpu.CompilerParams(vmem_limit_bytes=4 << 20),
    )(*in_vmem(*results), after)


def from_beside(at):
    return along_z(1 - 2 * at["core"])(at)


def rounded_sum(a, b):
    return (a.astype(jnp.float32) + b.astype(jnp.float32)).astype(a.dtype)


def exchange(weights, tokens, grad, fragment):
    own, give = pick(weights, fragment)
    partner = permute(give, flip("xl"))
    (sent,) = gate((tokens,), (partner,))
    after, across, before = (permute(sent, in_group(step)) for step in (1, 2, 3))
    gathered = lax.all_gather(lay(own, partner), "zh", axis=0, tiled=False)
    here = lax.all_gather(gathered, "core", axis=0, tiled=False)
    other = permute(grad, flip("xh"))
    mine, far = pack(permute(here, from_beside), grad, other, (after, across, before))
    far = permute(far, from_beside)
    theirs = permute(mine, flip("core"))
    far = lax.all_gather(far, "core", axis=0, tiled=False)
    total = unpack(mine, theirs, grad.shape)
    other = permute(total, flip("y"))
    outs = multiply((tokens, after, across, before), here, mine, theirs, far)
    total, other = gate((total, other), outs[1:])
    total = rounded_sum(total, other)
    results = [outs[0]] + [permute(outs[step], in_group(-step)) for step in (1, 2, 3)]
    total = rounded_sum(total, permute(total, flip("y", 2)))
    return results, total


def per_device(weights, momentum, pseudo_grad, tokens, fragment):
    results, total = exchange(weights, tokens, pseudo_grad[0], fragment)
    synced = lax.dynamic_index_in_dim(weights, fragment[0], 0, keepdims=False)
    replicas = lax.axis_size(REP)
    own_grad = pseudo_grad[0].astype(jnp.float32)
    averaged = total.astype(jnp.float32) / replicas
    velocity = MU * momentum.astype(jnp.float32) + averaged
    synced_wide = synced.astype(jnp.float32)
    outer_weights = synced_wide - OUTER_LR * (averaged + MU * velocity)
    inner_weights = synced_wide - own_grad
    blended = (MIX * inner_weights + (1.0 - MIX) * outer_weights).astype(jnp.bfloat16)
    new_momentum = velocity.astype(jnp.bfloat16)
    return (blended[None], new_momentum, assemble(results, new_momentum))


def solution(mesh):
    split = Mesh(mesh.devices.reshape(tuple(SIZES.values())), AXES)
    in_specs = (
        P(None, FSDP, None),
        P(FSDP, None),
        P(REP, FSDP, None),
        P(REP + FSDP, None),
        P(),
    )
    out_specs = (P(REP, FSDP, None), P(FSDP, None), P(REP + FSDP, None))
    return jax.shard_map(
        per_device, mesh=split, in_specs=in_specs, out_specs=out_specs, check_vma=False
    )
```

```python
import jax
import jax.numpy as jnp
from jax import lax
from jax.experimental import pallas as pl
from jax.experimental.pallas import tpu as pltpu
from jax.sharding import Mesh, PartitionSpec as P

MU = 0.9
OUTER_LR = 0.7
MIX = 0.5

SIZES = {"xh": 2, "y": 4, "core": 2, "zh": 4, "zl": 4, "xl": 2}
AXES = tuple(SIZES)
REP = ("xh", "y", "core")
FSDP = ("zh", "zl", "xl")
CHIPS = 4
PARTS = SIZES["zl"]

ANY = pl.BlockSpec(memory_space=pl.ANY)
WHOLE = pl.BlockSpec(memory_space=pltpu.VMEM)


def in_vmem(*values):
    return [pltpu.with_memory_space_constraint(value, pltpu.VMEM) for value in values]


def in_hbm(*values):
    return [pltpu.with_memory_space_constraint(value, pltpu.HBM) for value in values]


def vmem_like(shape, dtype=jnp.bfloat16):
    return pltpu.VMEM(shape, dtype)


SMALL = pltpu.CompilerParams(vmem_limit_bytes=1 << 20)


def permute(value, move):
    pairs = []
    total = 1
    for size in SIZES.values():
        total *= size
    for source in range(total):
        rest, at = source, {}
        for axis in reversed(AXES):
            at[axis] = rest % SIZES[axis]
            rest //= SIZES[axis]
        to = move(dict(at))
        target = 0
        for axis in AXES:
            target = target * SIZES[axis] + to[axis] % SIZES[axis]
        pairs.append((source, target))
    return lax.ppermute(value, AXES, pairs)


def along_z(step):
    def move(at):
        z = (at["zh"] * SIZES["zl"] + at["zl"] + step) % (SIZES["zh"] * SIZES["zl"])
        at["zh"], at["zl"] = divmod(z, SIZES["zl"])
        return at

    return move


def in_group(step):
    def move(at):
        if at["core"] == 0:
            at["y"] = (at["y"] + step) % SIZES["y"]
        else:
            x = (at["xh"] * SIZES["xl"] + at["xl"] + step) % (SIZES["xh"] * SIZES["xl"])
            at["xh"], at["xl"] = divmod(x, SIZES["xl"])
        return at

    return move


def flip(axis, bit=1):
    def move(at):
        at[axis] ^= bit
        return at

    return move


def quarter(xl):
    return lax.rem(lax.axis_index("xh") * SIZES["xl"] + xl + lax.axis_index("y"), CHIPS)


def pick(weights, fragment):
    rows, cols = weights.shape[1:]
    width = cols // (CHIPS * SIZES["core"])

    def kernel(fragment_ref, weights_ref, own_ref, give_ref, sems):
        xl = lax.axis_index("xl")
        core = lax.axis_index("core")
        copies = []
        for n, (ref, at) in enumerate(((own_ref, xl), (give_ref, 1 - xl))):
            start = pl.multiple_of((quarter(at) * SIZES["core"] + core) * width, 128)
            source = weights_ref.at[fragment_ref[1], :, pl.ds(start, width)]
            copies.append(pltpu.make_async_copy(source, ref, sems.at[n]))
        for copy in copies:
            copy.start()
        for copy in copies:
            copy.wait()

    return pl.pallas_call(
        kernel,
        out_shape=[vmem_like((rows, width))] * 2,
        in_specs=[pl.BlockSpec(memory_space=pltpu.SMEM), ANY],
        out_specs=[WHOLE] * 2,
        scratch_shapes=[pltpu.SemaphoreType.DMA((2,))],
        compiler_params=SMALL,
    )(fragment, *in_hbm(weights))


def lay(own, partner):
    rows, width = own.shape

    def kernel(own_ref, partner_ref, out_ref):
        xl = lax.axis_index("xl")
        for ref, at in ((own_ref, xl), (partner_ref, 1 - xl)):
            out_ref[pl.ds(pl.multiple_of(at * rows, 16), rows), :] = ref[...]

    return pl.pallas_call(
        kernel,
        out_shape=vmem_like((2 * rows, width)),
        in_specs=[WHOLE] * 2,
        out_specs=WHOLE,
        compiler_params=SMALL,
    )(*in_vmem(own, partner))


def gate(values, after):
    def kernel(*refs):
        del refs

    return pl.pallas_call(
        kernel,
        out_shape=[vmem_like(value.shape) for value in values],
        in_specs=[WHOLE] * len(values) + [ANY] * len(after),
        out_specs=[WHOLE] * len(values),
        input_output_aliases={n: n for n in range(len(values))},
        compiler_params=SMALL,
    )(*in_vmem(*values), *after)


def choose(value, after):
    def kernel(value_ref, *refs):
        refs[-1][...] = value_ref[lax.axis_index("core")]

    return pl.pallas_call(
        kernel,
        out_shape=vmem_like(value.shape[1:]),
        in_specs=[WHOLE] + [ANY] * len(after),
        out_specs=WHOLE,
        compiler_params=SMALL,
    )(*in_vmem(value), *after)


def multiply(blocks, here, mine, theirs, far):
    tokens, depth = blocks[0].shape
    halves, steps, rows, width = here.shape

    def kernel(*refs):
        token_refs, (here_ref, mine_ref, theirs_ref, far_ref) = refs[:CHIPS], refs[CHIPS : CHIPS + 4]
        out_refs, total = refs[CHIPS + 4 : -1], refs[-1]
        zl, core = lax.axis_index("zl"), lax.axis_index("core")
        step = pl.program_id(0)
        sets = ((here_ref, 0), (mine_ref, 3 - 2 * core), (theirs_ref, 1 + 2 * core), (far_ref, 2))
        for n, token_ref in enumerate(token_refs):
            part = None
            for ref, place in sets:
                weight = jnp.concatenate([ref[half, 0] for half in range(halves)], axis=1)
                plane = lax.rem(zl + place, PARTS)
                if n == 0:
                    plane += step * PARTS
                start = pl.multiple_of(plane * rows, 128)
                term = jnp.dot(
                    token_ref[:, pl.ds(start, rows)], weight, preferred_element_type=jnp.float32
                )
                part = term if part is None else part + term
            total[n] = jnp.where(step == 0, part, total[n] + part)

        @pl.when(step == steps - 1)
        def _():
            for n, out_ref in enumerate(out_refs):
                out_ref[...] = total[n].astype(out_ref.dtype)

    weight_spec = pl.BlockSpec((halves, 1, rows, width), lambda s: (0, s, 0, 0))
    token_spec = pl.BlockSpec((tokens, depth // steps), lambda s: (0, s))
    shape = (tokens, halves * width)
    return pl.pallas_call(
        kernel,
        grid=(steps,),
        out_shape=(vmem_like(shape),) * CHIPS,
        in_specs=[WHOLE] + [token_spec] * (CHIPS - 1) + [weight_spec] * 4,
        out_specs=(WHOLE,) * CHIPS,
        scratch_shapes=[pltpu.VMEM((CHIPS, *shape), jnp.float32)],
        compiler_params=pltpu.CompilerParams(vmem_limit_bytes=32 << 20),
        cost_estimate=pl.CostEstimate(
            flops=2 * CHIPS * tokens * depth * halves * width,
            bytes_accessed=2 * (CHIPS * tokens + halves * width) * depth,
            transcendentals=0,
        ),
    )(*in_vmem(blocks[0]), *blocks[1:], here, mine, theirs, far)


def assemble(results, after):
    tokens, width = results[0].shape

    def kernel(*refs):
        out_ref = refs[-1]
        first = quarter(lax.axis_index("xl"))
        for n, ref in enumerate(refs[:CHIPS]):
            start = pl.multiple_of(lax.rem(first + n, CHIPS) * width, 128)
            out_ref[:, pl.ds(start, width)] = ref[...]

    return pl.pallas_call(
        kernel,
        out_shape=jax.ShapeDtypeStruct((tokens, CHIPS * width), results[0].dtype),
        in_specs=[WHOLE] * CHIPS + [ANY],
        out_specs=WHOLE,
        compiler_params=pltpu.CompilerParams(vmem_limit_bytes=4 << 20),
    )(*in_vmem(*results), after)


def from_beside(at):
    return along_z(1 - 2 * at["core"])(at)


def beside_y(at):
    at["y"] = (at["y"] + 1 - 2 * at["core"]) % SIZES["y"]
    return at


def rounded_sum(a, b):
    return (a.astype(jnp.float32) + b.astype(jnp.float32)).astype(a.dtype)


def exchange(weights, tokens, grad, fragment):
    own, give = pick(weights, fragment)
    partner = permute(give, flip("xl"))
    (sent,) = gate((tokens,), (partner,))
    after, across, before = (permute(sent, in_group(step)) for step in (1, 2, 3))
    other = permute(grad, flip("core"))
    gathered = lax.all_gather(lay(own, partner), "zh", axis=0, tiled=False)
    here = lax.all_gather(gathered, "core", axis=0, tiled=False)
    mine = permute(here, from_beside)
    total = rounded_sum(grad, other)
    other = permute(total, flip("y", 2))
    far = permute(choose(mine, (after, across, before)), from_beside)
    theirs = permute(mine, flip("core"))
    far = lax.all_gather(far, "core", axis=0, tiled=False)
    total = rounded_sum(total, other)
    other = permute(total, beside_y)
    outs = multiply((tokens, after, across, before), here, mine, theirs, far)
    total, other = gate((total, other), outs[1:])
    total = rounded_sum(total, other)
    results = [outs[0]] + [permute(outs[step], in_group(-step)) for step in (1, 2, 3)]
    total = rounded_sum(total, permute(total, flip("xh")))
    return results, total


def per_device(weights, momentum, pseudo_grad, tokens, fragment):
    results, total = exchange(weights, tokens, pseudo_grad[0], fragment)
    synced = lax.dynamic_index_in_dim(weights, fragment[0], 0, keepdims=False)
    replicas = lax.axis_size(REP)
    own_grad = pseudo_grad[0].astype(jnp.float32)
    averaged = total.astype(jnp.float32) / replicas
    velocity = MU * momentum.astype(jnp.float32) + averaged
    synced_wide = synced.astype(jnp.float32)
    outer_weights = synced_wide - OUTER_LR * (averaged + MU * velocity)
    inner_weights = synced_wide - own_grad
    blended = (MIX * inner_weights + (1.0 - MIX) * outer_weights).astype(jnp.bfloat16)
    new_momentum = velocity.astype(jnp.bfloat16)
    return (blended[None], new_momentum, assemble(results, new_momentum))


def solution(mesh):
    split = Mesh(mesh.devices.reshape(tuple(SIZES.values())), AXES)
    in_specs = (
        P(None, FSDP, None),
        P(FSDP, None),
        P(REP, FSDP, None),
        P(REP + FSDP, None),
        P(),
    )
    out_specs = (P(REP, FSDP, None), P(FSDP, None), P(REP + FSDP, None))
    return jax.shard_map(
        per_device, mesh=split, in_specs=in_specs, out_specs=out_specs, check_vma=False
    )
```

```python
import jax
import jax.numpy as jnp
from jax import lax
from jax.experimental import pallas as pl
from jax.experimental.pallas import tpu as pltpu
from jax.sharding import Mesh, PartitionSpec as P

MU = 0.9
OUTER_LR = 0.7
MIX = 0.5

SIZES = {"xh": 2, "y": 4, "core": 2, "zh": 4, "zl": 4, "xl": 2}
AXES = tuple(SIZES)
REP = ("xh", "y", "core")
FSDP = ("zh", "zl", "xl")
CHIPS = 4
PARTS = SIZES["zl"]

ANY = pl.BlockSpec(memory_space=pl.ANY)
WHOLE = pl.BlockSpec(memory_space=pltpu.VMEM)


def in_vmem(*values):
    return [pltpu.with_memory_space_constraint(value, pltpu.VMEM) for value in values]


def in_hbm(*values):
    return [pltpu.with_memory_space_constraint(value, pltpu.HBM) for value in values]


def vmem_like(shape, dtype=jnp.bfloat16):
    return pltpu.VMEM(shape, dtype)


SMALL = pltpu.CompilerParams(vmem_limit_bytes=1 << 20)


def permute(value, move):
    pairs = []
    total = 1
    for size in SIZES.values():
        total *= size
    for source in range(total):
        rest, at = source, {}
        for axis in reversed(AXES):
            at[axis] = rest % SIZES[axis]
            rest //= SIZES[axis]
        to = move(dict(at))
        target = 0
        for axis in AXES:
            target = target * SIZES[axis] + to[axis] % SIZES[axis]
        pairs.append((source, target))
    return lax.ppermute(value, AXES, pairs)


def along_z(step):
    def move(at):
        z = (at["zh"] * SIZES["zl"] + at["zl"] + step) % (SIZES["zh"] * SIZES["zl"])
        at["zh"], at["zl"] = divmod(z, SIZES["zl"])
        return at

    return move


def in_group(step):
    def move(at):
        if at["core"] == 0:
            at["y"] = (at["y"] + step) % SIZES["y"]
        else:
            x = (at["xh"] * SIZES["xl"] + at["xl"] + step) % (SIZES["xh"] * SIZES["xl"])
            at["xh"], at["xl"] = divmod(x, SIZES["xl"])
        return at

    return move


def flip(axis, bit=1):
    def move(at):
        at[axis] ^= bit
        return at

    return move


def quarter(xl):
    return lax.rem(lax.axis_index("xh") * SIZES["xl"] + xl + lax.axis_index("y"), CHIPS)


def pick(weights, fragment):
    rows, cols = weights.shape[1:]
    width = cols // (CHIPS * SIZES["core"])

    def kernel(fragment_ref, weights_ref, own_ref, give_ref, sems):
        xl = lax.axis_index("xl")
        core = lax.axis_index("core")
        copies = []
        for n, (ref, at) in enumerate(((own_ref, xl), (give_ref, 1 - xl))):
            start = pl.multiple_of((quarter(at) * SIZES["core"] + core) * width, 128)
            source = weights_ref.at[fragment_ref[1], :, pl.ds(start, width)]
            copies.append(pltpu.make_async_copy(source, ref, sems.at[n]))
        for copy in copies:
            copy.start()
        for copy in copies:
            copy.wait()

    return pl.pallas_call(
        kernel,
        out_shape=[vmem_like((rows, width))] * 2,
        in_specs=[pl.BlockSpec(memory_space=pltpu.SMEM), ANY],
        out_specs=[WHOLE] * 2,
        scratch_shapes=[pltpu.SemaphoreType.DMA((2,))],
        compiler_params=SMALL,
    )(fragment, *in_hbm(weights))


def lay(own, partner):
    rows, width = own.shape

    def kernel(own_ref, partner_ref, out_ref):
        xl = lax.axis_index("xl")
        for ref, at in ((own_ref, xl), (partner_ref, 1 - xl)):
            out_ref[pl.ds(pl.multiple_of(at * rows, 16), rows), :] = ref[...]

    return pl.pallas_call(
        kernel,
        out_shape=vmem_like((2 * rows, width)),
        in_specs=[WHOLE] * 2,
        out_specs=WHOLE,
        compiler_params=SMALL,
    )(*in_vmem(own, partner))


def gate(values, after):
    def kernel(*refs):
        del refs

    return pl.pallas_call(
        kernel,
        out_shape=[vmem_like(value.shape) for value in values],
        in_specs=[WHOLE] * len(values) + [ANY] * len(after),
        out_specs=[WHOLE] * len(values),
        input_output_aliases={n: n for n in range(len(values))},
        compiler_params=SMALL,
    )(*in_vmem(*values), *after)


def choose(value, after):
    def kernel(value_ref, *refs):
        refs[-1][...] = value_ref[lax.axis_index("core")]

    return pl.pallas_call(
        kernel,
        out_shape=vmem_like(value.shape[1:]),
        in_specs=[WHOLE] + [ANY] * len(after),
        out_specs=WHOLE,
        compiler_params=SMALL,
    )(*in_vmem(value), *after)


def multiply(blocks, here, mine, theirs, far):
    tokens, depth = blocks[0].shape
    halves, steps, rows, width = here.shape

    def kernel(*refs):
        token_refs, (here_ref, mine_ref, theirs_ref, far_ref) = refs[:CHIPS], refs[CHIPS : CHIPS + 4]
        out_refs, total = refs[CHIPS + 4 : -1], refs[-1]
        zl, core = lax.axis_index("zl"), lax.axis_index("core")
        step = pl.program_id(0)
        sets = ((here_ref, 0), (mine_ref, 3 - 2 * core), (theirs_ref, 1 + 2 * core), (far_ref, 2))
        for n, token_ref in enumerate(token_refs):
            part = None
            for ref, place in sets:
                weight = jnp.concatenate([ref[half, 0] for half in range(halves)], axis=1)
                plane = lax.rem(zl + place, PARTS)
                if n == 0:
                    plane += step * PARTS
                start = pl.multiple_of(plane * rows, 128)
                term = jnp.dot(
                    token_ref[:, pl.ds(start, rows)], weight, preferred_element_type=jnp.float32
                )
                part = term if part is None else part + term
            total[n] = jnp.where(step == 0, part, total[n] + part)

        @pl.when(step == steps - 1)
        def _():
            for n, out_ref in enumerate(out_refs):
                out_ref[...] = total[n].astype(out_ref.dtype)

    weight_spec = pl.BlockSpec((halves, 1, rows, width), lambda s: (0, s, 0, 0))
    token_spec = pl.BlockSpec((tokens, depth // steps), lambda s: (0, s))
    shape = (tokens, halves * width)
    return pl.pallas_call(
        kernel,
        grid=(steps,),
        out_shape=(vmem_like(shape),) * CHIPS,
        in_specs=[WHOLE] + [token_spec] * (CHIPS - 1) + [weight_spec] * 4,
        out_specs=(WHOLE,) * CHIPS,
        scratch_shapes=[pltpu.VMEM((CHIPS, *shape), jnp.float32)],
        compiler_params=pltpu.CompilerParams(vmem_limit_bytes=32 << 20),
        cost_estimate=pl.CostEstimate(
            flops=2 * CHIPS * tokens * depth * halves * width,
            bytes_accessed=2 * (CHIPS * tokens + halves * width) * depth,
            transcendentals=0,
        ),
    )(*in_vmem(blocks[0]), *blocks[1:], here, mine, theirs, far)


def assemble(results, after):
    tokens, width = results[0].shape

    def kernel(*refs):
        out_ref = refs[-1]
        first = quarter(lax.axis_index("xl"))
        for n, ref in enumerate(refs[:CHIPS]):
            start = pl.multiple_of(lax.rem(first + n, CHIPS) * width, 128)
            out_ref[:, pl.ds(start, width)] = ref[...]

    return pl.pallas_call(
        kernel,
        out_shape=jax.ShapeDtypeStruct((tokens, CHIPS * width), results[0].dtype),
        in_specs=[WHOLE] * CHIPS + [ANY],
        out_specs=WHOLE,
        compiler_params=pltpu.CompilerParams(vmem_limit_bytes=4 << 20),
    )(*in_vmem(*results), *in_hbm(after))


def from_beside(at):
    return along_z(1 - 2 * at["core"])(at)


def beside_y(at):
    at["y"] = (at["y"] + 1 - 2 * at["core"]) % SIZES["y"]
    return at


def rounded_sum(a, b):
    return (a.astype(jnp.float32) + b.astype(jnp.float32)).astype(a.dtype)


def exchange(weights, tokens, grad, fragment):
    own, give = pick(weights, fragment)
    partner = permute(give, flip("xl"))
    (sent,) = gate((tokens,), (partner,))
    after, across, before = (permute(sent, in_group(step)) for step in (1, 2, 3))
    other = permute(grad, flip("core"))
    gathered = lax.all_gather(lay(own, partner), "zh", axis=0, tiled=False)
    here = lax.all_gather(gathered, "core", axis=0, tiled=False)
    mine = permute(here, from_beside)
    total = rounded_sum(grad, other)
    other = permute(total, flip("y", 2))
    far = permute(choose(mine, (after, across, before)), from_beside)
    theirs = permute(mine, flip("core"))
    far = lax.all_gather(far, "core", axis=0, tiled=False)
    total = rounded_sum(total, other)
    other = permute(total, beside_y)
    outs = multiply((tokens, after, across, before), here, mine, theirs, far)
    total, other = gate((total, other), outs[1:])
    total = rounded_sum(total, other)
    results = [outs[0]] + [permute(outs[step], in_group(-step)) for step in (1, 2, 3)]
    return results, total, permute(total, flip("xh"))


def outer_step(weights, momentum, grad, total, other, fragment):
    rows, cols = grad.shape
    steps = 2
    replicas = lax.axis_size(REP)

    def kernel(fragment_ref, weights_ref, momentum_ref, grad_ref, total_ref, other_ref, blended_ref, velocity_ref):
        del fragment_ref
        averaged = (total_ref[...].astype(jnp.float32) + other_ref[...].astype(jnp.float32)) / replicas
        velocity = MU * momentum_ref[...].astype(jnp.float32) + averaged
        synced = weights_ref[0].astype(jnp.float32)
        outer_weights = synced - OUTER_LR * (averaged + MU * velocity)
        inner_weights = synced - grad_ref[...].astype(jnp.float32)
        blended = MIX * inner_weights + (1.0 - MIX) * outer_weights
        blended_ref[...] = blended.astype(blended_ref.dtype)
        velocity_ref[...] = velocity.astype(velocity_ref.dtype)

    block = pl.BlockSpec((rows // steps, cols), lambda n, fragment_ref: (n, 0))
    layer = pl.BlockSpec((1, rows // steps, cols), lambda n, fragment_ref: (fragment_ref[0], n, 0))
    return pl.pallas_call(
        kernel,
        grid_spec=pltpu.PrefetchScalarGridSpec(
            num_scalar_prefetch=1,
            grid=(steps,),
            in_specs=[layer] + [block] * 4,
            out_specs=[block] * 2,
        ),
        out_shape=[pltpu.HBM(grad.shape, grad.dtype)] * 2,
        compiler_params=pltpu.CompilerParams(vmem_limit_bytes=12 << 20),
    )(fragment, weights, momentum, grad, total, other)


def per_device(weights, momentum, pseudo_grad, tokens, fragment):
    results, total, other = exchange(weights, tokens, pseudo_grad[0], fragment)
    blended, new_momentum = outer_step(weights, momentum, pseudo_grad[0], total, other, fragment)
    return (blended[None], new_momentum, assemble(results, new_momentum))


def solution(mesh):
    split = Mesh(mesh.devices.reshape(tuple(SIZES.values())), AXES)
    in_specs = (
        P(None, FSDP, None),
        P(FSDP, None),
        P(REP, FSDP, None),
        P(REP + FSDP, None),
        P(),
    )
    out_specs = (P(REP, FSDP, None), P(FSDP, None), P(REP + FSDP, None))
    return jax.shard_map(
        per_device, mesh=split, in_specs=in_specs, out_specs=out_specs, check_vma=False
    )
```

```python
import jax
import jax.numpy as jnp
from jax import lax
from jax.experimental import pallas as pl
from jax.experimental.pallas import tpu as pltpu
from jax.sharding import Mesh, PartitionSpec as P

MU = 0.9
OUTER_LR = 0.7
MIX = 0.5

SIZES = {"xh": 2, "y": 4, "core": 2, "zh": 4, "zl": 4, "xl": 2}
AXES = tuple(SIZES)
REP = ("xh", "y", "core")
FSDP = ("zh", "zl", "xl")
CHIPS = 4
PARTS = SIZES["zl"]

ANY = pl.BlockSpec(memory_space=pl.ANY)
WHOLE = pl.BlockSpec(memory_space=pltpu.VMEM)


def in_vmem(*values):
    return [pltpu.with_memory_space_constraint(value, pltpu.VMEM) for value in values]


def in_hbm(*values):
    return [pltpu.with_memory_space_constraint(value, pltpu.HBM) for value in values]


def vmem_like(shape, dtype=jnp.bfloat16):
    return pltpu.VMEM(shape, dtype)


SMALL = pltpu.CompilerParams(vmem_limit_bytes=1 << 20)


def permute(value, move):
    pairs = []
    total = 1
    for size in SIZES.values():
        total *= size
    for source in range(total):
        rest, at = source, {}
        for axis in reversed(AXES):
            at[axis] = rest % SIZES[axis]
            rest //= SIZES[axis]
        to = move(dict(at))
        target = 0
        for axis in AXES:
            target = target * SIZES[axis] + to[axis] % SIZES[axis]
        pairs.append((source, target))
    return lax.ppermute(value, AXES, pairs)


def along_z(step):
    def move(at):
        z = (at["zh"] * SIZES["zl"] + at["zl"] + step) % (SIZES["zh"] * SIZES["zl"])
        at["zh"], at["zl"] = divmod(z, SIZES["zl"])
        return at

    return move


def in_group(step):
    def move(at):
        if at["core"] == 0:
            at["y"] = (at["y"] + step) % SIZES["y"]
        else:
            x = (at["xh"] * SIZES["xl"] + at["xl"] + step) % (SIZES["xh"] * SIZES["xl"])
            at["xh"], at["xl"] = divmod(x, SIZES["xl"])
        return at

    return move


def flip(axis, bit=1):
    def move(at):
        at[axis] ^= bit
        return at

    return move


def quarter(xl):
    return lax.rem(lax.axis_index("xh") * SIZES["xl"] + xl + lax.axis_index("y"), CHIPS)


def pick(weights, fragment):
    rows, cols = weights.shape[1:]
    width = cols // (CHIPS * SIZES["core"])

    def kernel(fragment_ref, weights_ref, own_ref, give_ref, sems):
        xl = lax.axis_index("xl")
        core = lax.axis_index("core")
        copies = []
        for n, (ref, at) in enumerate(((own_ref, xl), (give_ref, 1 - xl))):
            start = pl.multiple_of((quarter(at) * SIZES["core"] + core) * width, 128)
            source = weights_ref.at[fragment_ref[1], :, pl.ds(start, width)]
            copies.append(pltpu.make_async_copy(source, ref, sems.at[n]))
        for copy in copies:
            copy.start()
        for copy in copies:
            copy.wait()

    return pl.pallas_call(
        kernel,
        out_shape=[vmem_like((rows, width))] * 2,
        in_specs=[pl.BlockSpec(memory_space=pltpu.SMEM), ANY],
        out_specs=[WHOLE] * 2,
        scratch_shapes=[pltpu.SemaphoreType.DMA((2,))],
        compiler_params=SMALL,
    )(fragment, *in_hbm(weights))


def lay(own, partner):
    rows, width = own.shape

    def kernel(own_ref, partner_ref, out_ref):
        xl = lax.axis_index("xl")
        for ref, at in ((own_ref, xl), (partner_ref, 1 - xl)):
            out_ref[pl.ds(pl.multiple_of(at * rows, 16), rows), :] = ref[...]

    return pl.pallas_call(
        kernel,
        out_shape=vmem_like((2 * rows, width)),
        in_specs=[WHOLE] * 2,
        out_specs=WHOLE,
        compiler_params=SMALL,
    )(*in_vmem(own, partner))


def gate(values, after):
    def kernel(*refs):
        del refs

    return pl.pallas_call(
        kernel,
        out_shape=[vmem_like(value.shape) for value in values],
        in_specs=[WHOLE] * len(values) + [ANY] * len(after),
        out_specs=[WHOLE] * len(values),
        input_output_aliases={n: n for n in range(len(values))},
        compiler_params=SMALL,
    )(*in_vmem(*values), *after)


def choose(value, after):
    def kernel(value_ref, *refs):
        refs[-1][...] = value_ref[lax.axis_index("core")]

    return pl.pallas_call(
        kernel,
        out_shape=vmem_like(value.shape[1:]),
        in_specs=[WHOLE] + [ANY] * len(after),
        out_specs=WHOLE,
        compiler_params=SMALL,
    )(*in_vmem(value), *after)


def multiply(blocks, here, mine, theirs, far):
    tokens, depth = blocks[0].shape
    halves, steps, rows, width = here.shape

    def kernel(*refs):
        token_refs, (here_ref, mine_ref, theirs_ref, far_ref) = refs[:CHIPS], refs[CHIPS : CHIPS + 4]
        out_refs, total = refs[CHIPS + 4 : -1], refs[-1]
        zl, core = lax.axis_index("zl"), lax.axis_index("core")
        step = pl.program_id(0)
        sets = ((here_ref, 0), (mine_ref, 3 - 2 * core), (theirs_ref, 1 + 2 * core), (far_ref, 2))
        for n, token_ref in enumerate(token_refs):
            part = None
            for ref, place in sets:
                at = step if ref is far_ref else 0
                weight = jnp.concatenate([ref[half, at] for half in range(halves)], axis=1)
                plane = lax.rem(zl + place, PARTS)
                if n == 0:
                    plane += step * PARTS
                start = pl.multiple_of(plane * rows, 128)
                term = jnp.dot(
                    token_ref[:, pl.ds(start, rows)], weight, preferred_element_type=jnp.float32
                )
                part = term if part is None else part + term
            total[n] = jnp.where(step == 0, part, total[n] + part)

        @pl.when(step == steps - 1)
        def _():
            for n, out_ref in enumerate(out_refs):
                out_ref[...] = total[n].astype(out_ref.dtype)

    weight_spec = pl.BlockSpec((halves, 1, rows, width), lambda s: (0, s, 0, 0))
    token_spec = pl.BlockSpec((tokens, depth // steps), lambda s: (0, s))
    shape = (tokens, halves * width)
    return pl.pallas_call(
        kernel,
        grid=(steps,),
        out_shape=(vmem_like(shape),) * CHIPS,
        in_specs=[WHOLE] + [token_spec] * (CHIPS - 1) + [weight_spec] * 3 + [WHOLE],
        out_specs=(WHOLE,) * CHIPS,
        scratch_shapes=[pltpu.VMEM((CHIPS, *shape), jnp.float32)],
        compiler_params=pltpu.CompilerParams(vmem_limit_bytes=32 << 20),
        cost_estimate=pl.CostEstimate(
            flops=2 * CHIPS * tokens * depth * halves * width,
            bytes_accessed=2 * (CHIPS * tokens + halves * width) * depth,
            transcendentals=0,
        ),
    )(*in_vmem(blocks[0]), *blocks[1:], here, mine, theirs, *in_vmem(far))


def assemble(results, after):
    tokens, width = results[0].shape

    def kernel(*refs):
        out_ref = refs[-1]
        first = quarter(lax.axis_index("xl"))
        for n, ref in enumerate(refs[:CHIPS]):
            start = pl.multiple_of(lax.rem(first + n, CHIPS) * width, 128)
            out_ref[:, pl.ds(start, width)] = ref[...]

    return pl.pallas_call(
        kernel,
        out_shape=jax.ShapeDtypeStruct((tokens, CHIPS * width), results[0].dtype),
        in_specs=[WHOLE] * CHIPS + [ANY],
        out_specs=WHOLE,
        compiler_params=pltpu.CompilerParams(vmem_limit_bytes=4 << 20),
    )(*in_vmem(*results), after)


def from_beside(at):
    return along_z(1 - 2 * at["core"])(at)


def beside_y(at):
    at["y"] = (at["y"] + 1 - 2 * at["core"]) % SIZES["y"]
    return at


def rounded_sum(a, b):
    return (a.astype(jnp.float32) + b.astype(jnp.float32)).astype(a.dtype)


def exchange(weights, tokens, grad, fragment):
    own, give = pick(weights, fragment)
    partner = permute(give, flip("xl"))
    (sent,) = gate((tokens,), (partner,))
    after, across, before = (permute(sent, in_group(step)) for step in (1, 2, 3))
    other = permute(grad, flip("core"))
    gathered = lax.all_gather(lay(own, partner), "zh", axis=0, tiled=False)
    here = lax.all_gather(gathered, "core", axis=0, tiled=False)
    mine = permute(here, from_beside)
    total = rounded_sum(grad, other)
    other = permute(total, flip("y", 2))
    far = permute(choose(mine, (after, across, before)), from_beside)
    theirs = permute(mine, flip("core"))
    far = lax.all_gather(far, "core", axis=0, tiled=False)
    total = rounded_sum(total, other)
    other = permute(total, beside_y)
    outs = multiply((tokens, after, across, before), here, mine, theirs, far)
    total, other = gate((total, other), outs[1:])
    total = rounded_sum(total, other)
    results = [outs[0]] + [permute(outs[step], in_group(-step)) for step in (1, 2, 3)]
    total = rounded_sum(total, permute(total, flip("xh")))
    return results, total


def per_device(weights, momentum, pseudo_grad, tokens, fragment):
    results, total = exchange(weights, tokens, pseudo_grad[0], fragment)
    synced = lax.dynamic_index_in_dim(weights, fragment[0], 0, keepdims=False)
    replicas = lax.axis_size(REP)
    own_grad = pseudo_grad[0].astype(jnp.float32)
    averaged = total.astype(jnp.float32) / replicas
    velocity = MU * momentum.astype(jnp.float32) + averaged
    synced_wide = synced.astype(jnp.float32)
    outer_weights = synced_wide - OUTER_LR * (averaged + MU * velocity)
    inner_weights = synced_wide - own_grad
    blended = (MIX * inner_weights + (1.0 - MIX) * outer_weights).astype(jnp.bfloat16)
    new_momentum = velocity.astype(jnp.bfloat16)
    return (blended[None], new_momentum, assemble(results, new_momentum))


def solution(mesh):
    split = Mesh(mesh.devices.reshape(tuple(SIZES.values())), AXES)
    in_specs = (
        P(None, FSDP, None),
        P(FSDP, None),
        P(REP, FSDP, None),
        P(REP + FSDP, None),
        P(),
    )
    out_specs = (P(REP, FSDP, None), P(FSDP, None), P(REP + FSDP, None))
    return jax.shard_map(
        per_device, mesh=split, in_specs=in_specs, out_specs=out_specs, check_vma=False
    )
```
